32 devices in a mesh: cell: 2 (over y), row: 16 (over z, x, core).
Axes of the slice: x: 2, y: 2, z: 4, core: 2. Of those that a mesh axis runs over, the one named last changes fastest.
Arguments:
- e_blocks: bfloat16 [128, 4, 128, 128], P(('cell', 'row')), parts along dimension 0, may hold values from -0.0625 to 0.0625
- e_cols: int32 [128, 4], P('cell'), parts along dimension 0, may hold values from 0 to 63, as said below
- p1_blocks: bfloat16 [128, 4, 128, 128], P(('cell', 'row')), parts along dimension 0, may hold values from -6 to 6
- p1_cols: int32 [128, 4], P('cell'), parts along dimension 0, may hold values from 0 to 63, as said below
- dh_owned: bfloat16 [384, 128, 128], P(('cell', 'row')), parts along dimension 0, may hold values from -6 to 6
- dh_source: int32 [128, 3], P(('cell', 'row')), parts along dimension 0, may hold values from 0 to 191, as said below
- dh_slot: int32 [128, 3], P(('cell', 'row')), parts along dimension 0, may hold values from 0 to 3, as said below
Outputs:
- e_out: float32 [128, 4, 128, 128], P(('cell', 'row')), parts along dimension 0
- p1_out: float32 [128, 4, 128, 128], P(('cell', 'row')), parts along dimension 0
The draws below stay inside these ranges and needn't reach their ends.
There are 2 independent parts, one for each index of `cell`. The reference program is written for one: setup_inputs(seed, part) draws one part's arguments, and reference() takes and returns one part's arrays. A program takes and returns all parts, laid end to end along the dimension named above; each array names one. Nothing has to cross between parts.
Inputs may be any that keep to these rules, and one draw needn't show every extreme that they name: `e_cols`: in every block row i the 4 columns are distinct and lie within 4 block rows of i, cyclically modulo 64; both offsets -4 and +4 occur. `p1_cols`: in every block row i the 4 columns are distinct and lie within 4 block rows of i, cyclically modulo 64; both offsets -4 and +4 occur. `dh_source`: A permutation of the owner-order positions. Owner-order position q lies on device q // 12; the block of block row i comes from the device of row i or from one of its two neighbours along the axis (cyclically), each device owning as many blocks of its own rows as of each neighbour's. `dh_slot`: the 3 slots of a block row are distinct.
All inputs are finite; a program needn't handle non-finite values.
Results may differ from the reference program's by a relative error of at most 0.00088.
Values may be sent and summed in bfloat16 or wider, within the bound.
A program may use at most 64 MiB of HBM per device.

```python
import math
import jax
import jax.numpy as jnp
from jax import lax

BLK = 128
BR_DEV = 4
REACH = 4
KB = 4
KD = 3
ITERS = 2
NBR = 64


def band_pattern(key):
    band_width = 2 * REACH + 1
    columns = jnp.arange(band_width, dtype=jnp.int32)[None, :]
    scores = jax.random.randint(key, (NBR, band_width), 0, 1 << 20, dtype=jnp.int32) * band_width + columns
    first_row = (jnp.arange(NBR, dtype=jnp.int32)[:, None] == 0) & ((columns == 0) | (columns == band_width - 1))
    scores = jnp.where(first_row, -1 - columns, scores)
    ranked = jnp.argsort(scores, axis=1)[:, :KB].astype(jnp.int32)
    offsets = ranked - REACH
    return ((jnp.arange(NBR, dtype=jnp.int32)[:, None] + offsets) % NBR).astype(jnp.int32)


def draw_e_cols(key, part):
    key = jax.random.fold_in(key, 11)
    return band_pattern(key)


def draw_p1_cols(key, part):
    key = jax.random.fold_in(key, 12)
    return band_pattern(key)


def draw_dh_slot(key, part):
    key = jax.random.fold_in(key, 13)
    columns = jnp.arange(KB, dtype=jnp.int32)[None, :]
    scores = jax.random.randint(key, (NBR, KB), 0, 1 << 20, dtype=jnp.int32) * KB + columns
    return jnp.argsort(scores, axis=1)[:, :KD].astype(jnp.int32)


def draw_dh_source(key, part):
    key = jax.random.fold_in(key, 14)
    owned_count = BR_DEV * KD
    third_count = owned_count // 3
    devices = NBR // BR_DEV
    key_first, key_second = jax.random.split(key)
    columns = jnp.arange(owned_count, dtype=jnp.int32)[None, :]
    first_scores = jax.random.randint(key_first, (devices, owned_count), 0, 1 << 20, dtype=jnp.int32) * owned_count + columns
    second_scores = jax.random.randint(key_second, (devices, owned_count), 0, 1 << 20, dtype=jnp.int32) * owned_count + columns
    first_perm = jnp.argsort(first_scores, axis=1).astype(jnp.int32)
    second_perm = jnp.argsort(second_scores, axis=1).astype(jnp.int32)
    group_id = first_perm // third_count
    step_dev = jnp.where(group_id == 1, 1, jnp.where(group_id == 2, -1, 0)).astype(jnp.int32)
    device_ids = jnp.arange(devices, dtype=jnp.int32)[:, None]
    owner_dev = (device_ids + step_dev) % devices
    slot_pos = group_id * third_count + first_perm % third_count
    final_slot = second_perm[owner_dev, slot_pos]
    source = owner_dev * owned_count + final_slot
    return source.reshape(NBR, KD).astype(jnp.int32)


def level_of(own_key, dims, cuts, smallest, top_value):
    factor_of, own = 1.0, jax.random.fold_in(own_key, 6)
    for dim, blocks in cuts:
        draws = jnp.exp(jax.random.uniform(jax.random.fold_in(own, dim), (blocks,), jnp.float32, smallest / len(cuts), top_value / len(cuts)))
        factor_of = factor_of * jnp.repeat(draws, dims[dim] // blocks).reshape([-1 if axis == dim else 1 for axis in range(len(dims))])
    return factor_of


def noise(key, dims, width, reach, cuts=(), kind=jnp.bfloat16):
    array = jax.random.normal(key, dims, jnp.float32) * width
    if len(cuts) > 0:
        array = level_of(key, dims, cuts, -0.22, 0.18) * array
    return jnp.clip(array, min=-reach, max=reach).astype(kind)


def setup_inputs(seed: int = 0, part: int = 0) -> dict:
    key_list = jax.random.split(jax.random.key(seed), 8)
    part_keys = jax.random.split(jax.random.fold_in(key_list[7], part), 8)
    e_blocks = noise(part_keys[0], (NBR, KB, BLK, BLK), (16 * KB * BLK) ** -0.5, 0.0625, ((0, 16),))
    e_cols = draw_e_cols(jax.random.fold_in(jax.random.fold_in(key_list[7], part), 71), part)
    p1_blocks = noise(part_keys[2], (NBR, KB, BLK, BLK), 1.0, 6.0, ((0, 16),))
    p1_cols = draw_p1_cols(jax.random.fold_in(jax.random.fold_in(key_list[7], part), 71), part)
    dh_owned = noise(part_keys[4], (NBR * KD, BLK, BLK), 1.0, 6.0, ((0, 16),))
    dh_source = draw_dh_source(jax.random.fold_in(jax.random.fold_in(key_list[7], part), 71), part)
    dh_slot = draw_dh_slot(jax.random.fold_in(jax.random.fold_in(key_list[7], part), 71), part)
    return {"e_blocks": e_blocks, "e_cols": e_cols, "p1_blocks": p1_blocks, "p1_cols": p1_cols, "dh_owned": dh_owned, "dh_source": dh_source, "dh_slot": dh_slot}


def multiply(left_blocks, left_cols, right_blocks, right_cols, target_cols):
    total_rows, right_count = right_cols.shape
    block_size = right_blocks.shape[-1]
    flat_right = right_blocks.reshape(-1, block_size, block_size)
    groups = total_rows // BR_DEV

    def one_group(inputs):
        group_blocks, group_cols, group_target = inputs
        held_cols = jnp.take(right_cols, group_cols, axis=0)
        matches = held_cols[:, :, :, None] == group_target[:, None, None, :]
        present = jnp.any(matches, axis=2)
        positions = jnp.arange(right_count, dtype=jnp.int32)[None, None, :, None]
        slot_pos = lax.optimization_barrier(jnp.sum(jnp.where(matches, positions, jnp.zeros((), jnp.int32)), axis=2)).astype(jnp.int32)
        flat_pos = (group_cols[:, :, None] * right_count + slot_pos).astype(jnp.int32)
        picked = jnp.take(flat_right, flat_pos, axis=0)
        picked = jnp.where(present[:, :, :, None, None], picked, jnp.zeros((), picked.dtype))
        return jnp.einsum('rkab,rknbc->rnac', group_blocks.astype(jnp.float32), picked.astype(jnp.float32))
    shaped = (left_blocks.reshape((groups, BR_DEV) + left_blocks.shape[1:]), left_cols.reshape(groups, BR_DEV, -1), target_cols.reshape(groups, BR_DEV, -1))
    result = lax.map(one_group, shaped)
    return result.reshape((total_rows, target_cols.shape[1], block_size, block_size))

def reference(e_blocks, e_cols, p1_blocks, p1_cols, dh_owned, dh_source, dh_slot):
    dh_rows = jnp.take(dh_owned, dh_source, axis=0)
    slot_table = (dh_slot[:, :, None] == jnp.arange(KB, dtype=jnp.int32)[None, None, :]).astype(jnp.float32)
    response = p1_blocks.astype(jnp.float32) + jnp.einsum('rum,ruab->rmab', slot_table, dh_rows.astype(jnp.float32))
    deviation = e_blocks.astype(jnp.float32)
    for iteration in range(ITERS):
        deviation_half = deviation.astype(jnp.bfloat16)
        response_half = response.astype(jnp.bfloat16)
        square = multiply(deviation_half, e_cols, deviation_half, e_cols, e_cols).astype(jnp.bfloat16)
        cube_term = multiply(square, e_cols, deviation_half, e_cols, e_cols)
        left_product = multiply(deviation_half, e_cols, response_half, p1_cols, p1_cols).astype(jnp.bfloat16)
        middle = multiply(left_product, p1_cols, deviation_half, e_cols, p1_cols)
        front_term = multiply(square, e_cols, response_half, p1_cols, p1_cols)
        back_term = multiply(response_half, p1_cols, square, e_cols, p1_cols)
        response = 1.5 * response - 2.0 * (front_term + middle + back_term)
        deviation = 1.5 * deviation - 2.0 * cube_term
    return (deviation * math.sqrt(KB * BLK), response)
```

```python
import functools
import math

import jax
import jax.numpy as jnp
from jax import lax
from jax.experimental import pallas as pl
from jax.experimental.pallas import tpu as pltpu
from jax.sharding import PartitionSpec as P

BLK = 128
REACH = 4
KB = 4
KD = 3
F32 = jnp.float32
BF16 = jnp.bfloat16
MESH = pl.DeviceIdType.MESH
VMEM_BYTES = 40 * 1024 * 1024


def kernel(
    total_rows,
    devices,
    e_cols,
    p1_cols,
    dh_source,
    dh_slot,
    source_hbm,
    e_hbm,
    p1_hbm,
    dh_hbm,
    e_out,
    p1_out,
    dev_wide,
    resp_wide,
    square_wide,
    next_wide,
    next_square,
    next_resp,
    left_prod,
    resp_f32,
    next_f32,
    p1_own,
    dh_own,
    dh_near,
    stage,
    source_vmem,
    source_smem,
    table,
    e_stage,
    p1_stage,
    local_sem,
    send_sem,
    recv_sem,
):
    rows = REACH
    own = rows * KB
    owned = rows * KD
    me = lax.axis_index("row")
    above = lax.rem(me + 1, devices)
    below = lax.rem(me + devices - 1, devices)
    row_start = me * rows

    def local(src, dst, sem):
        return pltpu.make_async_copy(src, dst, local_sem.at[sem])

    def remote(src, dst, sem, target):
        return pltpu.make_async_remote_copy(
            src_ref=src,
            dst_ref=dst,
            send_sem=send_sem.at[sem],
            recv_sem=recv_sem.at[sem],
            device_id={"row": target},
            device_id_type=MESH,
        )

    get_e = local(e_hbm, dev_wide.at[pl.ds(2 * own, own)], 0)
    get_p1 = local(p1_hbm, p1_own, 1)
    get_dh = local(dh_hbm, dh_own, 2)
    get_near = local(dh_hbm, dh_near.at[pl.ds(4, owned)], 3)
    get_e.start()
    get_dh.start()
    get_p1.start()
    get_near.start()

    barrier = pltpu.get_barrier_semaphore()
    for neighbour in (below, above):
        pl.semaphore_signal(
            barrier, inc=1, device_id={"row": neighbour}, device_id_type=MESH
        )
    pl.semaphore_wait(barrier, 2)

    src_up = remote(source_hbm, source_vmem.at[0], 0, above)
    src_down = remote(source_hbm, source_vmem.at[1], 1, below)
    src_up.start()
    src_down.start()
    dev_up = remote(e_hbm, dev_wide.at[pl.ds(own, own)], 2, above)
    dev_down = remote(e_hbm, dev_wide.at[pl.ds(3 * own, own)], 3, below)
    dev_up.start()
    dev_down.start()

    zero = jnp.zeros((BLK, BLK), BF16)
    dev_wide[4 * own] = zero
    for ref in (resp_wide, square_wide, next_wide, next_square, next_resp):
        ref[3 * own] = zero
    dh_near[owned + 8] = zero

    src_up.wait()
    src_down.wait()
    for side in range(2):
        to_smem = local(source_vmem.at[side], source_smem.at[side], 4 + side)
        to_smem.start()
        to_smem.wait()
    get_dh.wait()

    def fill_stage(side):
        count = jnp.int32(0)
        picked = [jnp.int32(0)] * 4
        for row in range(rows):
            for u in range(KD):
                position = source_smem[side, row, u]
                mine = lax.div(position, owned) == me
                here = position - me * owned
                for slot in range(4):
                    hit = jnp.logical_and(mine, count == slot)
                    picked[slot] = jnp.where(hit, here, picked[slot])
                count = count + jnp.where(mine, 1, 0)
        for slot in range(4):
            stage[side, slot] = dh_own[picked[slot]]

    fill_stage(0)
    fill_stage(1)
    dh_down = remote(stage.at[0], dh_near.at[pl.ds(owned + 4, 4)], 4, below)
    dh_up = remote(stage.at[1], dh_near.at[pl.ds(0, 4)], 5, above)
    dh_down.start()
    dh_up.start()

    def fill(base, first_row, left, right, target, low, high):
        def one(i, carry):
            row = lax.rem(row_start + first_row + i + total_rows, total_rows)
            wanted = [target[row, n] for n in range(KB)]
            for k in range(KB):
                col = left[row, k]
                near = lax.rem(col - row_start + 2 * REACH + total_rows, total_rows)
                start = near * KB + jnp.where(near >= 4 * REACH, 1, 0)
                held = [right[col, m] for m in range(KB)]
                for n in range(KB):
                    at = jnp.int32(4 * own)
                    for m in range(KB):
                        at = jnp.where(held[m] == wanted[n], start + m, at)
                    table[base + i * KB * KB + k * KB + n] = jnp.clip(at, low, high)
            return carry

        return one

    ee, ee_own, ep, pe = (rows_before * KB * KB for rows_before in (0, 12, 16, 20))
    lax.fori_loop(0, 12, fill(ee, -REACH, e_cols, e_cols, e_cols, 0, 5 * own), 0)
    for base, left, right, target in (
        (ee_own, e_cols, e_cols, e_cols),
        (ep, e_cols, p1_cols, p1_cols),
        (pe, p1_cols, e_cols, p1_cols),
    ):
        lax.fori_loop(0, 4, fill(base, 0, left, right, target, own, 4 * own), 0)

    dev_up.wait()
    dev_down.wait()
    fwd_up = remote(
        dev_wide.at[pl.ds(own, own)], dev_wide.at[pl.ds(0, own)], 6, above
    )
    fwd_down = remote(
        dev_wide.at[pl.ds(3 * own, own)], dev_wide.at[pl.ds(4 * own + 1, own)], 7, below
    )
    fwd_up.start()
    fwd_down.start()

    get_p1.wait()
    get_near.wait()
    dh_down.wait()
    dh_up.wait()
    from_below, from_above = jnp.int32(0), jnp.int32(0)
    for row in range(rows):
        at = [jnp.int32(owned + 8)] * KB
        for u in range(KD):
            position = dh_source[row, u]
            owner = lax.div(position, owned)
            is_below, is_above = owner == below, owner == above
            place = jnp.where(
                is_below,
                from_below,
                jnp.where(is_above, owned + 4 + from_above, 4 + position - me * owned),
            )
            place = jnp.clip(place, 0, owned + 8)
            from_below = from_below + jnp.where(is_below, 1, 0)
            from_above = from_above + jnp.where(is_above, 1, 0)
            slot = dh_slot[row, u]
            for m in range(KB):
                at[m] = jnp.where(slot == m, place, at[m])
        for m in range(KB):
            q = row * KB + m
            value = p1_own[q].astype(F32) + dh_near[at[m]].astype(F32)
            resp_f32[q] = value
            resp_wide[own + q] = value.astype(BF16)
    resp_up = remote(resp_wide.at[pl.ds(own, own)], resp_wide.at[pl.ds(0, own)], 8, above)
    resp_down = remote(
        resp_wide.at[pl.ds(own, own)], resp_wide.at[pl.ds(2 * own, own)], 9, below
    )
    resp_up.start()
    resp_down.start()

    def product(i, terms, sink):
        for pair in range(KB // 2):
            acc = None
            for left, left_base, right, right_off, base in terms:
                for half in range(KB // 2):
                    ks = (2 * half, 2 * half + 1)
                    ns = (2 * pair, 2 * pair + 1)
                    a = jnp.concatenate([left[left_base + i * KB + k] for k in ks], axis=1)
                    b = jnp.concatenate(
                        [
                            jnp.concatenate(
                                [
                                    right[table[base + i * KB * KB + k * KB + n] - right_off]
                                    for n in ns
                                ],
                                axis=1,
                            )
                            for k in ks
                        ],
                        axis=0,
                    )
                    part = jnp.dot(a, b, preferred_element_type=F32)
                    acc = part if acc is None else acc + part
            for j in range(2):
                sink(i * KB + 2 * pair + j, acc[:, j * BLK : (j + 1) * BLK])

    def run(count, terms, sink):
        def one(i, carry):
            product(i, terms, sink)
            return carry

        lax.fori_loop(0, count, one, 0)

    get_e.wait()
    fwd_up.wait()
    fwd_down.wait()

    def to_square(q, value):
        square_wide[q] = value.astype(BF16)

    run(12, [(dev_wide, own, dev_wide, 0, ee)], to_square)

    def to_next(q, value):
        new = 1.5 * dev_wide[own + q].astype(F32) - 2.0 * value
        next_f32[q] = new
        next_wide[q] = new.astype(BF16)

    run(12, [(square_wide, 0, dev_wide, 0, ee)], to_next)

    def to_next_square(q, value):
        next_square[own + q] = value.astype(BF16)

    run(4, [(next_wide, own, next_wide, own, ee_own)], to_next_square)
    sq_up = remote(
        next_square.at[pl.ds(own, own)], next_square.at[pl.ds(0, own)], 10, above
    )
    sq_down = remote(
        next_square.at[pl.ds(own, own)], next_square.at[pl.ds(2 * own, own)], 11, below
    )
    sq_up.start()
    sq_down.start()

    resp_up.wait()
    resp_down.wait()

    def to_left(q, value):
        left_prod[q] = value.astype(BF16)

    run(4, [(dev_wide, 2 * own, resp_wide, own, ep)], to_left)

    def to_resp(q, value):
        new = 1.5 * resp_f32[q] - 2.0 * value
        resp_f32[q] = new
        next_resp[own + q] = new.astype(BF16)

    run(
        4,
        [
            (square_wide, own, resp_wide, own, ep),
            (left_prod, 0, dev_wide, 0, pe),
            (resp_wide, own, square_wide, own, pe),
        ],
        to_resp,
    )
    next_up = remote(next_resp.at[pl.ds(own, own)], next_resp.at[pl.ds(0, own)], 12, above)
    next_down = remote(
        next_resp.at[pl.ds(own, own)], next_resp.at[pl.ds(2 * own, own)], 13, below
    )
    next_up.start()
    next_down.start()

    def to_e(q, value):
        e_stage[q] = 1.5 * next_f32[own + q] - 2.0 * value

    run(4, [(next_square, own, next_wide, own, ee_own)], to_e)
    put_e = local(e_stage, e_out, 6)
    put_e.start()

    sq_up.wait()
    sq_down.wait()

    def to_back(q, value):
        resp_f32[q] = 1.5 * resp_f32[q] - 2.0 * value

    run(4, [(next_resp, own, next_square, own, pe)], to_back)

    next_up.wait()
    next_down.wait()
    run(4, [(next_wide, own, next_resp, own, ep)], to_left)

    def to_out(q, value):
        p1_stage[q] = 0.5 * resp_f32[q] - value

    run(
        4,
        [(next_square, own, next_resp, own, ep), (left_prod, 0, next_wide, own, pe)],
        to_out,
    )
    put_p1 = local(p1_stage, p1_out, 7)
    put_p1.start()
    put_e.wait()
    put_p1.wait()


def body(e_blocks, e_cols, p1_blocks, p1_cols, dh_owned, dh_source, dh_slot):
    rows, slots, blk = e_blocks.shape[:3]
    own = rows * slots
    owned = dh_owned.shape[0]
    total_rows = e_cols.shape[0]
    devices = lax.axis_size("row")
    smem = pl.BlockSpec(memory_space=pltpu.SMEM)
    hbm = pl.BlockSpec(memory_space=pl.ANY)

    def blocks(count, kind=BF16):
        return pltpu.VMEM((count, blk, blk), kind)

    shape = jax.ShapeDtypeStruct((own, blk, blk), F32)
    deviation, half_response = pl.pallas_call(
        functools.partial(kernel, total_rows, devices),
        out_shape=(shape, shape),
        in_specs=[smem] * 4 + [hbm] * 4,
        out_specs=(hbm, hbm),
        scratch_shapes=[
            blocks(5 * own + 1),
            blocks(3 * own + 1),
            blocks(3 * own + 1),
            blocks(3 * own + 1),
            blocks(3 * own + 1),
            blocks(3 * own + 1),
            blocks(own),
            blocks(own, F32),
            blocks(3 * own, F32),
            blocks(own),
            blocks(owned),
            blocks(owned + 9),
            pltpu.VMEM((2, 4, blk, blk), BF16),
            pltpu.VMEM((2,) + dh_source.shape, jnp.int32),
            pltpu.SMEM((2,) + dh_source.shape, jnp.int32),
            pltpu.SMEM((24 * slots * slots,), jnp.int32),
            blocks(own, F32),
            blocks(own, F32),
            pltpu.SemaphoreType.DMA((8,)),
            pltpu.SemaphoreType.DMA((14,)),
            pltpu.SemaphoreType.DMA((14,)),
        ],
        compiler_params=pltpu.CompilerParams(
            collective_id=0, has_side_effects=True, vmem_limit_bytes=VMEM_BYTES
        ),
        cost_estimate=pl.CostEstimate(
            flops=16 * 2 * own * slots * blk**3, bytes_accessed=4 * 2**20, transcendentals=0
        ),
        name="purify",
    )(
        e_cols,
        p1_cols,
        dh_source,
        dh_slot,
        dh_source,
        e_blocks.reshape(own, blk, blk),
        p1_blocks.reshape(own, blk, blk),
        dh_owned,
    )
    e_out = deviation * math.sqrt(KB * BLK)
    p1_out = half_response * 2.0
    return (e_out.reshape(e_blocks.shape), p1_out.reshape(p1_blocks.shape))


def solution(mesh):
    in_specs = (
        P(("cell", "row"), None, None, None),
        P("cell", None),
        P(("cell", "row"), None, None, None),
        P("cell", None),
        P(("cell", "row"), None, None),
        P(("cell", "row"), None),
        P(("cell", "row"), None),
    )
    out_specs = (P(("cell", "row"), None, None, None), P(("cell", "row"), None, None, None))
    return jax.shard_map(body, mesh=mesh, in_specs=in_specs, out_specs=out_specs, check_vma=False)
```

```python
import functools
import math

import jax
import jax.numpy as jnp
from jax import lax
from jax.experimental import pallas as pl
from jax.experimental.pallas import tpu as pltpu
from jax.sharding import PartitionSpec as P

BLK = 128
REACH = 4
KB = 4
KD = 3
F32 = jnp.float32
BF16 = jnp.bfloat16
MESH = pl.DeviceIdType.MESH
CHUNKS = 2
N_REMOTE = 7 + 8 * CHUNKS
VMEM_BYTES = 56 * 1024 * 1024


def kernel(
    total_rows,
    devices,
    e_cols,
    p1_cols,
    dh_source,
    dh_slot,
    source_hbm,
    e_hbm,
    p1_hbm,
    dh_hbm,
    e_out,
    p1_out,
    dev_wide,
    resp_wide,
    square_wide,
    next_wide,
    next_square,
    next_resp,
    left_prod,
    resp_f32,
    next_f32,
    p1_own,
    dh_own,
    dh_near,
    stage,
    source_vmem,
    source_smem,
    table,
    e_stage,
    p1_stage,
    local_sem,
    send_sem,
    recv_sem,
):
    rows = REACH
    own = rows * KB
    owned = rows * KD
    wide = 7 * own
    centre = 3 * own
    me = lax.axis_index("row")
    core = lax.rem(me, 2)
    odd = lax.rem(lax.div(me, 2), 2)

    def device(step):
        return lax.rem(me + step + devices, devices)

    above, below = device(1), device(-1)
    cross, to_mate = 2 - 4 * odd, 1 - 2 * core
    mate, pair, onward = device(to_mate), device(cross), device(2 * cross)
    backward, diag, far = device(-2 * cross), device(-to_mate), device(6 * core - 3)

    def local(src, dst, sem):
        return pltpu.make_async_copy(src, dst, local_sem.at[sem])

    sems = iter(range(N_REMOTE))

    def remote(src, dst, target):
        sem = next(sems)
        return pltpu.make_async_remote_copy(
            src_ref=src,
            dst_ref=dst,
            send_sem=send_sem.at[sem],
            recv_sem=recv_sem.at[sem],
            device_id={"row": target},
            device_id_type=MESH,
        )

    def at_slot(ref, step, chunk=0, chunks=1):
        size = own // chunks
        return ref.at[pl.ds(centre + step * own + chunk * size, size)]

    get_e = local(e_hbm, at_slot(dev_wide, 0), 0)
    get_p1 = local(p1_hbm, p1_own, 1)
    get_dh = local(dh_hbm, dh_own, 2)
    get_near = local(dh_hbm, dh_near.at[pl.ds(4, owned)], 3)
    get_e.start()
    get_dh.start()
    get_p1.start()
    get_near.start()

    barrier = pltpu.get_barrier_semaphore()
    for neighbour in (mate, pair, onward, backward, diag, far):
        pl.semaphore_signal(
            barrier, inc=1, device_id={"row": neighbour}, device_id_type=MESH
        )
    pl.semaphore_wait(barrier, 6)

    src_up = remote(source_hbm, source_vmem.at[0], above)
    src_down = remote(source_hbm, source_vmem.at[1], below)
    src_up.start()
    src_down.start()

    class Spread:
        def __init__(self, ref, src, reach_far):
            self.ref, self.waits = ref, []
            size = own // CHUNKS
            self.crossing = [
                remote(
                    src(c * size, size), at_slot(ref, -cross, c, CHUNKS), pair
                )
                for c in range(CHUNKS)
            ]
            self.others = [remote(src(0, own), at_slot(ref, -to_mate), mate)]
            if reach_far:
                self.others.append(
                    remote(src(0, own), at_slot(ref, 3 - 6 * core), far)
                )
            for copy in self.crossing + self.others:
                copy.start()
            self.passed = []

        def pass_on(self, c):
            ref = self.ref
            self.crossing[c].wait_recv()
            held = at_slot(ref, cross, c, CHUNKS)
            passed = remote(held, at_slot(ref, -cross, c, CHUNKS), onward)
            shared = remote(held, at_slot(ref, cross - to_mate, c, CHUNKS), mate)
            passed.start()
            shared.start()
            self.passed.append(passed)
            self.others.append(shared)

        def share(self, c):
            ref = self.ref
            self.passed[c].wait_recv()
            shared = remote(
                at_slot(ref, -cross, c, CHUNKS),
                at_slot(ref, -cross - to_mate, c, CHUNKS),
                mate,
            )
            shared.start()
            self.others.append(shared)

        def finish(self):
            for copy in self.crossing + self.passed:
                copy.wait_send()
            for copy in self.others:
                copy.wait()

    dev = Spread(dev_wide, lambda first, size: e_hbm.at[pl.ds(first, size)], True)

    zero = jnp.zeros((BLK, BLK), BF16)
    for ref in (dev_wide, resp_wide, square_wide, next_wide, next_square, next_resp):
        ref[wide] = zero
    dh_near[owned + 8] = zero

    src_up.wait()
    src_down.wait()
    for side in range(2):
        to_smem = local(source_vmem.at[side], source_smem.at[side], 4 + side)
        to_smem.start()
        to_smem.wait()
    get_dh.wait()

    def fill_stage(side):
        count = jnp.int32(0)
        picked = [jnp.int32(0)] * 4
        for row in range(rows):
            for u in range(KD):
                position = source_smem[side, row, u]
                mine = lax.div(position, owned) == me
                here = position - me * owned
                for slot in range(4):
                    hit = jnp.logical_and(mine, count == slot)
                    picked[slot] = jnp.where(hit, here, picked[slot])
                count = count + jnp.where(mine, 1, 0)
        for slot in range(4):
            stage[side, slot] = dh_own[picked[slot]]

    fill_stage(0)
    fill_stage(1)
    dh_down = remote(stage.at[0], dh_near.at[pl.ds(owned + 4, 4)], below)
    dh_up = remote(stage.at[1], dh_near.at[pl.ds(0, 4)], above)
    dh_down.start()
    dh_up.start()

    def fill(base, left, right, target):
        def one(i, carry):
            row = lax.rem(row_start - 3 * REACH + i + total_rows, total_rows)
            wanted = [target[row, n] for n in range(KB)]
            for k in range(KB):
                col = left[row, k]
                near = lax.rem(col - row_start + 3 * REACH + total_rows, total_rows)
                held = [right[col, m] for m in range(KB)]
                for n in range(KB):
                    at = jnp.int32(wide)
                    for m in range(KB):
                        at = jnp.where(held[m] == wanted[n], near * KB + m, at)
                    table[base + i * KB * KB + k * KB + n] = jnp.clip(at, 0, wide)
            return carry

        return one

    row_start = me * rows
    ee, ep, pe = (kind * wide * KB for kind in range(3))
    lax.fori_loop(4, 24, fill(ee, e_cols, e_cols, e_cols), 0)
    for c in range(CHUNKS):
        dev.pass_on(c)

    get_p1.wait()
    get_near.wait()
    dh_down.wait()
    dh_up.wait()
    from_below, from_above = jnp.int32(0), jnp.int32(0)
    for row in range(rows):
        at = [jnp.int32(owned + 8)] * KB
        for u in range(KD):
            position = dh_source[row, u]
            owner = lax.div(position, owned)
            is_below, is_above = owner == below, owner == above
            place = jnp.where(
                is_below,
                from_below,
                jnp.where(is_above, owned + 4 + from_above, 4 + position - me * owned),
            )
            place = jnp.clip(place, 0, owned + 8)
            from_below = from_below + jnp.where(is_below, 1, 0)
            from_above = from_above + jnp.where(is_above, 1, 0)
            slot = dh_slot[row, u]
            for m in range(KB):
                at[m] = jnp.where(slot == m, place, at[m])
        for m in range(KB):
            q = row * KB + m
            value = p1_own[q].astype(F32) + dh_near[at[m]].astype(F32)
            resp_f32[q] = value
            resp_wide[centre + q] = value.astype(BF16)
    resp = Spread(
        resp_wide, lambda first, size: resp_wide.at[pl.ds(centre + first, size)], False
    )
    lax.fori_loop(8, 20, fill(ep, e_cols, p1_cols, p1_cols), 0)
    lax.fori_loop(8, 20, fill(pe, p1_cols, e_cols, p1_cols), 0)
    for c in range(CHUNKS):
        dev.share(c)

    def product(i, terms, sink):
        for pair_n in range(KB // 2):
            acc = None
            for left, right, base in terms:
                for half in range(KB // 2):
                    ks = (2 * half, 2 * half + 1)
                    ns = (2 * pair_n, 2 * pair_n + 1)
                    a = jnp.concatenate([left[i * KB + k] for k in ks], axis=1)
                    b = jnp.concatenate(
                        [
                            jnp.concatenate(
                                [right[table[base + i * KB * KB + k * KB + n]] for n in ns],
                                axis=1,
                            )
                            for k in ks
                        ],
                        axis=0,
                    )
                    part = jnp.dot(a, b, preferred_element_type=F32)
                    acc = part if acc is None else acc + part
            for j in range(2):
                sink(i * KB + 2 * pair_n + j, acc[:, j * BLK : (j + 1) * BLK])

    def run(first, last, terms, sink):
        def one(i, carry):
            product(i, terms, sink)
            return carry

        lax.fori_loop(first, last, one, 0)

    get_e.wait()
    dev.finish()

    def into(ref):
        def sink(q, value):
            ref[q] = value.astype(BF16)

        return sink

    run(4, 24, [(dev_wide, dev_wide, ee)], into(square_wide))

    def to_next(q, value):
        next_wide[q] = (1.5 * dev_wide[q].astype(F32) - 2.0 * value).astype(BF16)

    def to_next_own(q, value):
        new = 1.5 * dev_wide[q].astype(F32) - 2.0 * value
        next_f32[q - centre] = new
        next_wide[q] = new.astype(BF16)

    cube = [(square_wide, dev_wide, ee)]
    resp.pass_on(0)
    run(4, 12, cube, to_next)
    for c in range(1, CHUNKS):
        resp.pass_on(c)
    run(12, 16, cube, to_next_own)
    run(16, 24, cube, to_next)
    run(8, 20, [(next_wide, next_wide, ee)], into(next_square))

    def to_e(q, value):
        e_stage[q - centre] = 1.5 * next_f32[q - centre] - 2.0 * value

    run(12, 16, [(next_square, next_wide, ee)], to_e)
    put_e = local(e_stage, e_out, 6)
    put_e.start()
    for c in range(CHUNKS):
        resp.share(c)
    resp.finish()

    run(8, 20, [(dev_wide, resp_wide, ep)], into(left_prod))

    def to_resp(q, value):
        next_resp[q] = (1.5 * resp_wide[q].astype(F32) - 2.0 * value).astype(BF16)

    def to_resp_own(q, value):
        new = 1.5 * resp_f32[q - centre] - 2.0 * value
        resp_f32[q - centre] = new
        next_resp[q] = new.astype(BF16)

    terms = [
        (square_wide, resp_wide, ep),
        (left_prod, dev_wide, pe),
        (resp_wide, square_wide, pe),
    ]
    run(8, 12, terms, to_resp)
    run(12, 16, terms, to_resp_own)
    run(16, 20, terms, to_resp)

    run(12, 16, [(next_wide, next_resp, ep)], into(left_prod))

    def to_out(q, value):
        p1_stage[q - centre] = 0.75 * resp_f32[q - centre] - value

    run(
        12,
        16,
        [
            (next_square, next_resp, ep),
            (left_prod, next_wide, pe),
            (next_resp, next_square, pe),
        ],
        to_out,
    )
    put_p1 = local(p1_stage, p1_out, 7)
    put_p1.start()
    put_e.wait()
    put_p1.wait()


def body(e_blocks, e_cols, p1_blocks, p1_cols, dh_owned, dh_source, dh_slot):
    rows, slots, blk = e_blocks.shape[:3]
    own = rows * slots
    owned = dh_owned.shape[0]
    total_rows = e_cols.shape[0]
    devices = lax.axis_size("row")
    smem = pl.BlockSpec(memory_space=pltpu.SMEM)
    hbm = pl.BlockSpec(memory_space=pltpu.HBM)

    def blocks(count, kind=BF16):
        return pltpu.VMEM((count, blk, blk), kind)

    shape = jax.ShapeDtypeStruct((own, blk, blk), F32)
    deviation, half_response = pl.pallas_call(
        functools.partial(kernel, total_rows, devices),
        out_shape=(shape, shape),
        in_specs=[smem] * 4 + [hbm] * 4,
        out_specs=(hbm, hbm),
        scratch_shapes=[
            *[blocks(7 * own + 1)] * 6,
            blocks(7 * own),
            blocks(own, F32),
            blocks(own, F32),
            blocks(own),
            blocks(owned),
            blocks(owned + 9),
            pltpu.VMEM((2, 4, blk, blk), BF16),
            pltpu.VMEM((2,) + dh_source.shape, jnp.int32),
            pltpu.SMEM((2,) + dh_source.shape, jnp.int32),
            pltpu.SMEM((3 * 7 * own * slots,), jnp.int32),
            blocks(own, F32),
            blocks(own, F32),
            pltpu.SemaphoreType.DMA((8,)),
            pltpu.SemaphoreType.DMA((N_REMOTE,)),
            pltpu.SemaphoreType.DMA((N_REMOTE,)),
        ],
        compiler_params=pltpu.CompilerParams(
            collective_id=0, has_side_effects=True, vmem_limit_bytes=VMEM_BYTES
        ),
        cost_estimate=pl.CostEstimate(
            flops=30 * 2 * own * slots * blk**3, bytes_accessed=4 * 2**20, transcendentals=0
        ),
        name="purify",
    )(
        e_cols,
        p1_cols,
        dh_source,
        dh_slot,
        dh_source,
        e_blocks.reshape(own, blk, blk),
        p1_blocks.reshape(own, blk, blk),
        dh_owned,
    )
    e_out = deviation * math.sqrt(KB * BLK)
    p1_out = half_response * 2.0
    return (e_out.reshape(e_blocks.shape), p1_out.reshape(p1_blocks.shape))


def solution(mesh):
    in_specs = (
        P(("cell", "row"), None, None, None),
        P("cell", None),
        P(("cell", "row"), None, None, None),
        P("cell", None),
        P(("cell", "row"), None, None),
        P(("cell", "row"), None),
        P(("cell", "row"), None),
    )
    out_specs = (P(("cell", "row"), None, None, None), P(("cell", "row"), None, None, None))
    return jax.shard_map(body, mesh=mesh, in_specs=in_specs, out_specs=out_specs, check_vma=False)
```

```python
import functools
import math

import jax
import jax.numpy as jnp
from jax import lax
from jax.experimental import pallas as pl
from jax.experimental.pallas import tpu as pltpu
from jax.sharding import PartitionSpec as P

BLK = 128
REACH = 4
KB = 4
KD = 3
F32 = jnp.float32
BF16 = jnp.bfloat16
MESH = pl.DeviceIdType.MESH
CHUNKS = 2
UNROLL = 4
N_REMOTE = 7 + 8 * CHUNKS
VMEM_BYTES = 56 * 1024 * 1024


def kernel(
    total_rows,
    devices,
    e_cols,
    p1_cols,
    dh_source,
    dh_slot,
    source_hbm,
    e_hbm,
    p1_hbm,
    dh_hbm,
    e_out,
    p1_out,
    dev_wide,
    resp_wide,
    square_wide,
    next_wide,
    next_square,
    next_resp,
    left_prod,
    resp_f32,
    next_f32,
    p1_own,
    dh_own,
    dh_near,
    stage,
    source_vmem,
    source_smem,
    table,
    e_stage,
    p1_stage,
    local_sem,
    send_sem,
    recv_sem,
):
    rows = REACH
    own = rows * KB
    owned = rows * KD
    wide = 7 * own
    centre = 3 * own
    me = lax.axis_index("row")
    core = lax.rem(me, 2)
    odd = lax.rem(lax.div(me, 2), 2)

    def device(step):
        return lax.rem(me + step + devices, devices)

    above, below = device(1), device(-1)
    cross, to_mate = 2 - 4 * odd, 1 - 2 * core
    mate, pair, onward = device(to_mate), device(cross), device(2 * cross)
    backward, diag, far = device(-2 * cross), device(-to_mate), device(6 * core - 3)

    def local(src, dst, sem):
        return pltpu.make_async_copy(src, dst, local_sem.at[sem])

    sems = iter(range(N_REMOTE))

    def remote(src, dst, target):
        sem = next(sems)
        return pltpu.make_async_remote_copy(
            src_ref=src,
            dst_ref=dst,
            send_sem=send_sem.at[sem],
            recv_sem=recv_sem.at[sem],
            device_id={"row": target},
            device_id_type=MESH,
        )

    def at_slot(ref, step, chunk=0, chunks=1):
        size = own // chunks
        return ref.at[pl.ds(centre + step * own + chunk * size, size)]

    get_e = local(e_hbm, at_slot(dev_wide, 0), 0)
    get_p1 = local(p1_hbm, p1_own, 1)
    get_dh = local(dh_hbm, dh_own, 2)
    get_near = local(dh_hbm, dh_near.at[pl.ds(4, owned)], 3)
    get_e.start()
    get_dh.start()
    get_p1.start()
    get_near.start()

    barrier = pltpu.get_barrier_semaphore()
    for neighbour in (mate, pair, onward, backward, diag, far):
        pl.semaphore_signal(
            barrier, inc=1, device_id={"row": neighbour}, device_id_type=MESH
        )
    pl.semaphore_wait(barrier, 6)

    src_up = remote(source_hbm, source_vmem.at[0], above)
    src_down = remote(source_hbm, source_vmem.at[1], below)
    src_up.start()
    src_down.start()

    class Spread:
        def __init__(self, ref, src, reach_far):
            self.ref, self.waits = ref, []
            size = own // CHUNKS
            self.crossing = [
                remote(
                    src(c * size, size), at_slot(ref, -cross, c, CHUNKS), pair
                )
                for c in range(CHUNKS)
            ]
            self.others = [remote(src(0, own), at_slot(ref, -to_mate), mate)]
            if reach_far:
                self.others.append(
                    remote(src(0, own), at_slot(ref, 3 - 6 * core), far)
                )
            for copy in self.crossing + self.others:
                copy.start()
            self.passed = []

        def pass_on(self, c):
            ref = self.ref
            self.crossing[c].wait_recv()
            held = at_slot(ref, cross, c, CHUNKS)
            passed = remote(held, at_slot(ref, -cross, c, CHUNKS), onward)
            shared = remote(held, at_slot(ref, cross - to_mate, c, CHUNKS), mate)
            passed.start()
            shared.start()
            self.passed.append(passed)
            self.others.append(shared)

        def share(self, c):
            ref = self.ref
            self.passed[c].wait_recv()
            shared = remote(
                at_slot(ref, -cross, c, CHUNKS),
                at_slot(ref, -cross - to_mate, c, CHUNKS),
                mate,
            )
            shared.start()
            self.others.append(shared)

        def finish(self):
            for copy in self.crossing + self.passed:
                copy.wait_send()
            for copy in self.others:
                copy.wait()

    dev = Spread(dev_wide, lambda first, size: e_hbm.at[pl.ds(first, size)], True)

    zero = jnp.zeros((BLK, BLK), BF16)
    for ref in (dev_wide, resp_wide, square_wide, next_wide, next_square, next_resp):
        ref[wide] = zero
    dh_near[owned + 8] = zero

    src_up.wait()
    src_down.wait()
    for side in range(2):
        to_smem = local(source_vmem.at[side], source_smem.at[side], 4 + side)
        to_smem.start()
        to_smem.wait()
    get_dh.wait()

    def fill_stage(side):
        count = jnp.int32(0)
        picked = [jnp.int32(0)] * 4
        for row in range(rows):
            for u in range(KD):
                position = source_smem[side, row, u]
                here = position - me * owned
                mine = jnp.logical_and(here >= 0, here < owned)
                for slot in range(4):
                    hit = jnp.logical_and(mine, count == slot)
                    picked[slot] = jnp.where(hit, here, picked[slot])
                count = count + jnp.where(mine, 1, 0)
        for slot in range(4):
            stage[side, slot] = dh_own[picked[slot]]

    fill_stage(0)
    fill_stage(1)
    dh_down = remote(stage.at[0], dh_near.at[pl.ds(owned + 4, 4)], below)
    dh_up = remote(stage.at[1], dh_near.at[pl.ds(0, 4)], above)
    dh_down.start()
    dh_up.start()

    def around(row):
        row = jnp.where(row < 0, row + total_rows, row)
        return jnp.where(row >= total_rows, row - total_rows, row)

    def fill(base, left, right, target):
        def one(i, carry):
            row = around(row_start - 3 * REACH + i)
            wanted = [target[row, n] for n in range(KB)]
            for k in range(KB):
                col = left[row, k]
                start = around(col - row_start + 3 * REACH) * KB
                held = [right[col, m] for m in range(KB)]
                for n in range(KB):
                    at = jnp.int32(wide)
                    for m in range(KB):
                        at = jnp.where(held[m] == wanted[n], start + m, at)
                    table[base + i * KB * KB + k * KB + n] = jnp.clip(at, 0, wide)
            return carry

        return one

    row_start = me * rows
    ee, ep, pe = (kind * wide * KB for kind in range(3))
    for c in range(CHUNKS):
        dev.pass_on(c)

    get_p1.wait()
    get_near.wait()
    dh_down.wait()
    dh_up.wait()
    from_below, from_above = jnp.int32(0), jnp.int32(0)
    for row in range(rows):
        at = [jnp.int32(owned + 8)] * KB
        for u in range(KD):
            position = dh_source[row, u]
            in_below, in_above = position - below * owned, position - above * owned
            is_below = jnp.logical_and(in_below >= 0, in_below < owned)
            is_above = jnp.logical_and(in_above >= 0, in_above < owned)
            place = jnp.where(
                is_below,
                from_below,
                jnp.where(is_above, owned + 4 + from_above, 4 + position - me * owned),
            )
            place = jnp.clip(place, 0, owned + 8)
            from_below = from_below + jnp.where(is_below, 1, 0)
            from_above = from_above + jnp.where(is_above, 1, 0)
            slot = dh_slot[row, u]
            for m in range(KB):
                at[m] = jnp.where(slot == m, place, at[m])
        for m in range(KB):
            q = row * KB + m
            value = p1_own[q].astype(F32) + dh_near[at[m]].astype(F32)
            resp_f32[q] = value
            resp_wide[centre + q] = value.astype(BF16)
    resp = Spread(
        resp_wide, lambda first, size: resp_wide.at[pl.ds(centre + first, size)], False
    )
    lax.fori_loop(4, 24, fill(ee, e_cols, e_cols, e_cols), 0)
    lax.fori_loop(8, 20, fill(ep, e_cols, p1_cols, p1_cols), 0)
    lax.fori_loop(8, 20, fill(pe, p1_cols, e_cols, p1_cols), 0)
    for c in range(CHUNKS):
        dev.share(c)

    def product(i, terms, sink):
        for pair_n in range(KB // 2):
            acc = None
            for left, right, base in terms:
                for half in range(KB // 2):
                    ks = (2 * half, 2 * half + 1)
                    ns = (2 * pair_n, 2 * pair_n + 1)
                    a = jnp.concatenate([left[i * KB + k] for k in ks], axis=1)
                    b = jnp.concatenate(
                        [
                            jnp.concatenate(
                                [right[table[base + i * KB * KB + k * KB + n]] for n in ns],
                                axis=1,
                            )
                            for k in ks
                        ],
                        axis=0,
                    )
                    part = jnp.dot(a, b, preferred_element_type=F32)
                    acc = part if acc is None else acc + part
            for j in range(2):
                sink(i * KB + 2 * pair_n + j, acc[:, j * BLK : (j + 1) * BLK])

    def run(first, last, terms, sink):
        def one(i, carry):
            product(i, terms, sink)
            return carry

        lax.fori_loop(first, last, one, 0, unroll=UNROLL)

    get_e.wait()
    for c in range(CHUNKS):
        resp.pass_on(c)
    dev.finish()

    def into(ref):
        def sink(q, value):
            ref[q] = value.astype(BF16)

        return sink

    run(4, 24, [(dev_wide, dev_wide, ee)], into(square_wide))

    def to_next(q, value):
        next_wide[q] = (1.5 * dev_wide[q].astype(F32) - 2.0 * value).astype(BF16)

    def to_next_own(q, value):
        new = 1.5 * dev_wide[q].astype(F32) - 2.0 * value
        next_f32[q - centre] = new
        next_wide[q] = new.astype(BF16)

    cube = [(square_wide, dev_wide, ee)]
    run(4, 12, cube, to_next)
    run(12, 16, cube, to_next_own)
    run(16, 24, cube, to_next)
    run(8, 20, [(next_wide, next_wide, ee)], into(next_square))

    def to_e(q, value):
        e_stage[q - centre] = 1.5 * next_f32[q - centre] - 2.0 * value

    run(12, 16, [(next_square, next_wide, ee)], to_e)
    put_e = local(e_stage, e_out, 6)
    put_e.start()
    for c in range(CHUNKS):
        resp.share(c)
    resp.finish()

    run(8, 20, [(dev_wide, resp_wide, ep)], into(left_prod))

    def to_resp(q, value):
        next_resp[q] = (1.5 * resp_wide[q].astype(F32) - 2.0 * value).astype(BF16)

    def to_resp_own(q, value):
        new = 1.5 * resp_f32[q - centre] - 2.0 * value
        resp_f32[q - centre] = new
        next_resp[q] = new.astype(BF16)

    terms = [
        (square_wide, resp_wide, ep),
        (left_prod, dev_wide, pe),
        (resp_wide, square_wide, pe),
    ]
    run(8, 12, terms, to_resp)
    run(12, 16, terms, to_resp_own)
    run(16, 20, terms, to_resp)

    run(12, 16, [(next_wide, next_resp, ep)], into(left_prod))

    def to_out(q, value):
        p1_stage[q - centre] = 0.75 * resp_f32[q - centre] - value

    run(
        12,
        16,
        [
            (next_square, next_resp, ep),
            (left_prod, next_wide, pe),
            (next_resp, next_square, pe),
        ],
        to_out,
    )
    put_p1 = local(p1_stage, p1_out, 7)
    put_p1.start()
    put_e.wait()
    put_p1.wait()


def body(e_blocks, e_cols, p1_blocks, p1_cols, dh_owned, dh_source, dh_slot):
    rows, slots, blk = e_blocks.shape[:3]
    own = rows * slots
    owned = dh_owned.shape[0]
    total_rows = e_cols.shape[0]
    devices = lax.axis_size("row")
    smem = pl.BlockSpec(memory_space=pltpu.SMEM)
    hbm = pl.BlockSpec(memory_space=pltpu.HBM)

    def blocks(count, kind=BF16):
        return pltpu.VMEM((count, blk, blk), kind)

    shape = jax.ShapeDtypeStruct((own, blk, blk), F32)
    deviation, half_response = pl.pallas_call(
        functools.partial(kernel, total_rows, devices),
        out_shape=(shape, shape),
        in_specs=[smem] * 4 + [hbm] * 4,
        out_specs=(hbm, hbm),
        scratch_shapes=[
            *[blocks(7 * own + 1)] * 6,
            blocks(7 * own),
            blocks(own, F32),
            blocks(own, F32),
            blocks(own),
            blocks(owned),
            blocks(owned + 9),
            pltpu.VMEM((2, 4, blk, blk), BF16),
            pltpu.VMEM((2,) + dh_source.shape, jnp.int32),
            pltpu.SMEM((2,) + dh_source.shape, jnp.int32),
            pltpu.SMEM((3 * 7 * own * slots,), jnp.int32),
            blocks(own, F32),
            blocks(own, F32),
            pltpu.SemaphoreType.DMA((8,)),
            pltpu.SemaphoreType.DMA((N_REMOTE,)),
            pltpu.SemaphoreType.DMA((N_REMOTE,)),
        ],
        compiler_params=pltpu.CompilerParams(
            collective_id=0, has_side_effects=True, vmem_limit_bytes=VMEM_BYTES
        ),
        cost_estimate=pl.CostEstimate(
            flops=30 * 2 * own * slots * blk**3, bytes_accessed=4 * 2**20, transcendentals=0
        ),
        name="purify",
    )(
        e_cols,
        p1_cols,
        dh_source,
        dh_slot,
        dh_source,
        e_blocks.reshape(own, blk, blk),
        p1_blocks.reshape(own, blk, blk),
        dh_owned,
    )
    e_out = deviation * math.sqrt(KB * BLK)
    p1_out = half_response * 2.0
    return (e_out.reshape(e_blocks.shape), p1_out.reshape(p1_blocks.shape))


def solution(mesh):
    in_specs = (
        P(("cell", "row"), None, None, None),
        P("cell", None),
        P(("cell", "row"), None, None, None),
        P("cell", None),
        P(("cell", "row"), None, None),
        P(("cell", "row"), None),
        P(("cell", "row"), None),
    )
    out_specs = (P(("cell", "row"), None, None, None), P(("cell", "row"), None, None, None))
    return jax.shard_map(body, mesh=mesh, in_specs=in_specs, out_specs=out_specs, check_vma=False)
```
